768 devices in a mesh: row: 32 (over z_hi, y), col: 24 (over x, z_lo, core).
Axes of the slice: x: 4, y: 8, z: 12 (z_hi: 4, z_lo: 3; z = z_hi * 3 + z_lo), core: 2. Of those that a mesh axis runs over, the one named last changes fastest.
Arguments:
- features: bfloat16 [24, 4096, 128], P('col', 'row'), may hold values from -6 to 6
- out_degree: int32 [24, 4096], P('col', 'row'), may hold values from 8 to 96
- in_degree: int32 [32, 3072], P('row', 'col'), may hold values from 8 to 96
- tile_pos: int32 [32, 24, 32, 2], P('row', 'col'), may hold values from 0 to 15, as said below
- tile_count: int32 [32, 24], P('row', 'col'), may hold values from 1 to 32, as said below
- tiles: bfloat16 [32, 24, 32, 256, 256], P('row', 'col'), as said below
- weight: bfloat16 [128, 256], replicated, may hold values from -0.5 to 0.5
- cotangent: bfloat16 [32, 3072, 256], P('row', 'col'), may hold values from -0.076171875 to 0.076171875
Outputs:
- output: bfloat16 [32, 3072, 256], P('row', 'col')
- grad_weight: float32 [128, 256], replicated
The draws below stay inside these ranges and needn't reach their ends.
Inputs may be any that keep to these rules, and one draw needn't show every extreme that they name: `tile_pos`: each device's slots hold distinct tile positions of its block of 3072 x 4096 nodes, row tile first; slots from tile_count on hold positions too and are not used; some device's first slot is the block's last tile. `tile_count`: some device uses all 32 slots. `tiles`: nonnegative edge weights, zero where there is no edge; most entries of a tile are zero.
All inputs are finite; a program needn't handle non-finite values.
Results may differ from the reference program's by a relative error of at most 0.025.
Values may be sent and summed in bfloat16 or wider, within the bound.
No kernel may reach another device: no remote copies, remote signals or barrier semaphores. Data moves between devices by JAX's collectives and lax.ppermute only.
A program may use at most 32 MiB of HBM per device.

```python
import math
import jax
import jax.numpy as jnp
from jax import lax

CH = 128
F = 256
TILE = 256
NODE_DEV = 128
ROWNODES = 3072
COLNODES = 4096
NODES = 98304
TILES_DEV = 32
N_ROW = 32
N_COL = 24


def draw_tile_pos(key, part):
    key = jax.random.fold_in(key, 11)
    row_tiles = ROWNODES // TILE
    col_tiles = COLNODES // TILE
    places = row_tiles * col_tiles
    devices = N_ROW * N_COL
    device_keys = jax.random.split(key, devices)
    orders = jax.vmap(lambda single: jax.random.permutation(single, places))(device_keys)
    chosen = jax.random.randint(jax.random.fold_in(key, 1), (), 0, devices)
    rotated = (orders - orders[:, :1] + places - 1) % places
    orders = jnp.where((jnp.arange(devices) == chosen)[:, None], rotated, orders)
    picked = orders[:, :TILES_DEV]
    stacked = jnp.stack([picked // col_tiles, picked % col_tiles], -1)
    return stacked.reshape(N_ROW, N_COL, TILES_DEV, 2).astype(jnp.int32)


def draw_tile_count(key, part):
    key = jax.random.fold_in(key, 12)
    first = jax.random.randint(jax.random.fold_in(key, 1), (N_ROW * N_COL,), 1, TILES_DEV + 1)
    second = jax.random.randint(jax.random.fold_in(key, 2), (N_ROW * N_COL,), 1, TILES_DEV + 1)
    counts = jnp.minimum(first, second)
    chosen = jax.random.randint(jax.random.fold_in(key, 3), (), 0, N_ROW * N_COL)
    counts = jnp.where(jnp.arange(N_ROW * N_COL) == chosen, TILES_DEV, counts)
    return counts.reshape(N_ROW, N_COL).astype(jnp.int32)


def edge_values(key, low, high):
    shape = (N_ROW, N_COL, TILES_DEV, TILE, TILE)
    slots_entries = TILES_DEV * TILE * TILE
    share = max(0.01, min(0.5, 40.0 * NODE_DEV / slots_entries))
    present = (jax.random.uniform(jax.random.fold_in(key, 1), shape) < share).astype(jnp.float32)
    magnitude = jax.random.uniform(jax.random.fold_in(key, 2), shape, jnp.float32, low, high)
    scaling = 60.0 / math.sqrt(share * slots_entries / NODE_DEV)
    return (present * magnitude * scaling).astype(jnp.bfloat16)


def draw_tiles(key, part):
    key = jax.random.fold_in(key, 13)
    return edge_values(key, 0.5, 1.5)


def set_ends(drawn, rng, low, top_value):
    longest = drawn.shape.index(max(drawn.shape))
    spots = []
    for shift in (0, 1):
        where = [jax.random.randint(jax.random.fold_in(rng, axis), (), 0, length) for axis, length in enumerate(drawn.shape)]
        where[longest] = (where[longest] + shift) % drawn.shape[longest]
        spots.append(tuple(where))
    return drawn.at[spots[0]].set(low).at[spots[1]].set(top_value)


def shard_levels(rng, extent, shards, smallest, largest):
    def one(dim, shards_of):
        draws = jax.random.uniform(jax.random.fold_in(jax.random.fold_in(rng, 6), dim), (shards_of,), jnp.float32, smallest / len(shards), largest / len(shards))
        return jnp.repeat(jnp.exp(draws), extent[dim] // shards_of).reshape((-1,) + (1,) * (len(extent) - dim - 1))

    factor_of = one(*shards[0])
    for cut in shards[1:]:
        factor_of = factor_of * one(*cut)
    return factor_of


def noise(rng, shape, scale, bound, shards=(), dtype=jnp.bfloat16):
    result = scale * jax.random.normal(rng, shape, jnp.float32)
    if shards:
        result = result * shard_levels(rng, shape, shards, -0.22, 0.18)
    return jnp.clip(result, -bound, bound).astype(dtype)


def setup_inputs(seed: int = 0) -> dict:
    streams_of = jax.random.split(jax.random.key(seed), 9)
    features = noise(streams_of[0], (N_COL, COLNODES, CH), 1.0, 6.0, ((0, 24), (1, 32)))
    out_degree = set_ends(jax.random.randint(streams_of[1], (N_COL, COLNODES), 8, 97), jax.random.fold_in(streams_of[1], 1), 8, 96).astype(jnp.int32)
    in_degree = set_ends(jax.random.randint(streams_of[2], (N_ROW, ROWNODES), 8, 97), jax.random.fold_in(streams_of[2], 1), 8, 96).astype(jnp.int32)
    tile_pos = draw_tile_pos(jax.random.fold_in(streams_of[8], 71), 0)
    tile_count = draw_tile_count(jax.random.fold_in(streams_of[8], 71), 0)
    tiles = draw_tiles(jax.random.fold_in(streams_of[8], 71), 0)
    weight = noise(streams_of[6], (CH, F), CH ** -0.5, 0.5)
    cotangent = noise(streams_of[7], (N_ROW, ROWNODES, F), (4.0 / NODES ** 0.5), 0.076171875, ((0, 32), (1, 24)))
    return {"features": features, "out_degree": out_degree, "in_degree": in_degree, "tile_pos": tile_pos, "tile_count": tile_count, "tiles": tiles, "weight": weight, "cotangent": cotangent}


def device_term(tile_block, positions, live_count, source):
    blocks = source.reshape(COLNODES // TILE, TILE, CH)
    picked = blocks[positions[:, 1]]
    product = jnp.einsum('tij,tjk->tik', tile_block.astype(jnp.float32), picked.astype(jnp.float32), precision=lax.Precision.HIGHEST)
    live = jnp.arange(TILES_DEV).astype(jnp.int32) < live_count
    row_ids = jnp.arange(ROWNODES // TILE).astype(jnp.int32)
    select = ((positions[:, 0][None, :] == row_ids[:, None]) & live[None, :]).astype(jnp.float32)
    summed = jnp.einsum('rt,tik->rik', select, product, precision=lax.Precision.HIGHEST)
    return summed.reshape(ROWNODES, CH).astype(jnp.bfloat16)

def reference(features, out_degree, in_degree, tile_pos, tile_count, tiles, weight, cotangent):
    scaled = (features.astype(jnp.float32) * lax.rsqrt(out_degree.astype(jnp.float32))[..., None]).astype(jnp.bfloat16)

    def one_row(row_index):

        def add_column(total, column):
            term = device_term(tiles[row_index, column], tile_pos[row_index, column], tile_count[row_index, column], scaled[column])
            return (total + term.astype(jnp.float32), None)
        total, unused = lax.scan(add_column, jnp.zeros((ROWNODES, CH), jnp.float32), jnp.arange(N_COL).astype(jnp.int32))
        return total
    sums = lax.map(one_row, jnp.arange(N_ROW).astype(jnp.int32))
    aggregated = (sums * lax.rsqrt(in_degree.astype(jnp.float32))[..., None]).astype(jnp.bfloat16)
    flat = aggregated.reshape(-1, CH)
    output = jnp.dot(flat, weight, preferred_element_type=jnp.float32).astype(jnp.bfloat16).reshape(N_ROW, ROWNODES, F)
    grad_weight = jnp.dot(flat.T, cotangent.reshape(-1, F), preferred_element_type=jnp.float32)
    return (output, grad_weight)
```

```python
import jax
import jax.numpy as jnp
from jax import lax
from jax.experimental import pallas as pl
from jax.experimental.pallas import tpu as pltpu
from jax.sharding import Mesh, PartitionSpec as P

Z_HI, Y, X, Z_LO, CORE = 4, 8, 4, 3, 2
ROW = ("zh", "y")
COL = ("x", "zl", "core")
NODE = 128
TILE = 256
CH = 128
F = 256
ROW_TILES = X * Z_LO
N_COL = X * Z_LO * CORE
N_ROW = Z_HI * Y
PIECE = 11
UNROLL = 4


def tile_kernel(pos_ref, count_ref, core_ref, tiles_ref, source_ref, keep_ref, send_ref, acc_ref):
    count = count_ref[0]
    core = core_ref[0]
    slots = tiles_ref.shape[0]
    acc_ref[...] = jnp.zeros_like(acc_ref)

    def chunk(k, carry):
        products = []
        for u in range(UNROLL):
            s = k * UNROLL + u
            j = pos_ref[1, s]
            picked = source_ref[pl.ds(2 * (j % (Y // 2)), 2), j // (Y // 2)].reshape(TILE, CH)
            picked = jnp.where(s < count, picked, jnp.zeros_like(picked))
            products.append(jnp.dot(tiles_ref[s], picked, preferred_element_type=jnp.float32))
        for u in range(UNROLL):
            i = pos_ref[0, k * UNROLL + u]
            acc_ref[i] += products[u].reshape(CORE, NODE, CH)
        return carry

    lax.fori_loop(0, (count + UNROLL - 1) // UNROLL, chunk, 0)
    keep_ref[...] = acc_ref[:, core]
    send_ref[...] = acc_ref[:, 1 - core].astype(jnp.bfloat16)


def tile_product(positions, count, core, tiles, source):
    smem = pl.BlockSpec(memory_space=pltpu.SMEM)
    vmem = pl.BlockSpec(memory_space=pltpu.VMEM)
    return pl.pallas_call(
        tile_kernel,
        out_shape=(
            jax.ShapeDtypeStruct((ROW_TILES, NODE, CH), jnp.float32),
            jax.ShapeDtypeStruct((ROW_TILES, NODE, CH), jnp.bfloat16),
        ),
        in_specs=[smem, smem, smem, vmem, vmem],
        out_specs=(vmem, vmem),
        scratch_shapes=[pltpu.VMEM((ROW_TILES, CORE, NODE, CH), jnp.float32)],
        compiler_params=pltpu.CompilerParams(vmem_limit_bytes=32 * 1024 * 1024),
        cost_estimate=pl.CostEstimate(
            flops=2 * 32 * TILE * TILE * CH, bytes_accessed=8 * 1024 * 1024, transcendentals=0
        ),
        name="tile_product",
    )(positions, count, core, tiles, source)


def node_kernel(parts_ref, degree_ref, weight_ref, cot_ref, out_ref, grad_ref):
    total = jnp.sum(parts_ref[...].astype(jnp.float32), axis=0)
    aggregated = (total * lax.rsqrt(degree_ref[...].astype(jnp.float32))).astype(jnp.bfloat16)
    out_ref[...] = jnp.dot(
        aggregated, weight_ref[...], preferred_element_type=jnp.float32
    ).astype(jnp.bfloat16)
    grad = lax.dot_general(
        aggregated, cot_ref[...], (((0,), (0,)), ((), ())), preferred_element_type=jnp.float32
    )
    grad_ref[:CH] = grad[:, :CH]
    grad_ref[CH : 2 * CH] = grad[:, CH:]
    grad_ref[2 * CH :] = jnp.zeros_like(grad_ref[2 * CH :])


def node_stage(parts, degree, weight, cotangent):
    vmem = pl.BlockSpec(memory_space=pltpu.VMEM)
    return pl.pallas_call(
        node_kernel,
        out_shape=(
            jax.ShapeDtypeStruct((NODE, F), jnp.bfloat16),
            jax.ShapeDtypeStruct((N_COL * PIECE, CH), jnp.float32),
        ),
        in_specs=[vmem] * 4,
        out_specs=(vmem, vmem),
        name="node_stage",
    )(parts, degree, weight, cotangent)


def exchange(parts, axes):
    return lax.all_to_all(parts, axes, 0, 0)


def spread(piece, axes, n):
    return exchange(jnp.broadcast_to(piece[None], (n,) + piece.shape), axes)


def per_device(features, out_degree, in_degree, tile_pos, tile_count, tiles, weight, cotangent):
    core = lax.axis_index("core")
    scaled = (
        features[0].astype(jnp.float32) * lax.rsqrt(out_degree[0].astype(jnp.float32))[:, None]
    ).astype(jnp.bfloat16)
    over_z = lax.all_gather(scaled, "zh", axis=0)
    source = spread(over_z, "y", Y)

    keep, send = tile_product(
        tile_pos[0, 0].T, tile_count[0], core.reshape(1), tiles[0, 0], source
    )
    arrived = lax.ppermute(send, "core", [(0, 1), (1, 0)])
    pair = (keep + arrived.astype(jnp.float32)).astype(jnp.bfloat16)
    parts = exchange(pair, ("x", "zl"))

    output, local_grad = node_stage(parts, in_degree[0][:, None], weight, cotangent[0])

    piece = jnp.sum(exchange(local_grad.reshape(N_COL, PIECE, CH), COL), axis=0)
    piece = jnp.sum(spread(piece, ROW, N_ROW), axis=0)
    grad = spread(piece, COL, N_COL).reshape(N_COL * PIECE, CH)
    grad_weight = jnp.concatenate([grad[:CH], grad[CH : 2 * CH]], axis=1)
    return (output[None], grad_weight)


def solution(mesh):
    fine = Mesh(mesh.devices.reshape(Z_HI, Y, X, Z_LO, CORE), ROW + COL)
    return jax.shard_map(
        per_device,
        mesh=fine,
        in_specs=(
            P(COL, ROW, None),
            P(COL, ROW),
            P(ROW, COL),
            P(ROW, COL, None, None),
            P(ROW, COL),
            P(ROW, COL, None, None, None),
            P(),
            P(ROW, COL, None),
        ),
        out_specs=(P(ROW, COL, None), P()),
        check_vma=False,
    )
```

```python
import jax
import jax.numpy as jnp
from jax import lax
from jax.experimental import pallas as pl
from jax.experimental.pallas import tpu as pltpu
from jax.sharding import Mesh, PartitionSpec as P

Z_HI, Y, X, Z_LO, CORE = 4, 8, 4, 3, 2
ROW = ("zh", "y")
COL = ("x", "zl", "core")
NODE = 128
TILE = 256
CH = 128
F = 256
ROW_TILES = X * Z_LO
N_ROW = Z_HI * Y
PIECE = 32
UNROLL = 4


def tile_kernel(
    pos_ref, count_ref, core_ref, tiles_ref, source_ref, keep_ref, send_ref, acc_ref, held_ref, sems
):
    count = count_ref[0]
    core = core_ref[0]
    chunks = tiles_ref.shape[0] // UNROLL

    def fetch(k):
        slots = pl.ds(k * UNROLL, UNROLL)
        return pltpu.make_async_copy(tiles_ref.at[slots], held_ref.at[slots], sems.at[k])

    for k in range(chunks):
        fetch(k).start()
    acc_ref[...] = jnp.zeros_like(acc_ref)

    def chunk(k, carry):
        fetch(k).wait()

        @pl.when(k * UNROLL < count)
        def _():
            products = []
            for u in range(UNROLL):
                s = k * UNROLL + u
                j = pos_ref[1, s]
                picked = source_ref[pl.ds(2 * (j % (Y // 2)), 2), j // (Y // 2)].reshape(TILE, CH)
                picked = jnp.where(s < count, picked, jnp.zeros_like(picked))
                products.append(jnp.dot(held_ref[s], picked, preferred_element_type=jnp.float32))
            for u in range(UNROLL):
                i = pos_ref[0, k * UNROLL + u]
                acc_ref[i] += products[u].reshape(CORE, NODE, CH)

        return carry

    lax.fori_loop(0, chunks, chunk, 0)
    keep_ref[...] = acc_ref[:, core]
    send_ref[...] = acc_ref[:, 1 - core].astype(jnp.bfloat16)


def tile_product(positions, count, core, tiles, source):
    smem = pl.BlockSpec(memory_space=pltpu.SMEM)
    vmem = pl.BlockSpec(memory_space=pltpu.VMEM)
    return pl.pallas_call(
        tile_kernel,
        out_shape=(
            jax.ShapeDtypeStruct((ROW_TILES, NODE, CH), jnp.float32),
            jax.ShapeDtypeStruct((ROW_TILES, NODE, CH), jnp.bfloat16),
        ),
        in_specs=[smem, smem, smem, pl.BlockSpec(memory_space=pltpu.HBM), vmem],
        out_specs=(vmem, vmem),
        scratch_shapes=[
            pltpu.VMEM((ROW_TILES, CORE, NODE, CH), jnp.float32),
            pltpu.VMEM(tiles.shape, tiles.dtype),
            pltpu.SemaphoreType.DMA((tiles.shape[0] // UNROLL,)),
        ],
        compiler_params=pltpu.CompilerParams(vmem_limit_bytes=50 * 1024 * 1024),
        cost_estimate=pl.CostEstimate(
            flops=2 * 32 * TILE * TILE * CH, bytes_accessed=8 * 1024 * 1024, transcendentals=0
        ),
        name="tile_product",
    )(positions, count, core, tiles, source)


def pair_kernel(place_ref, keep_ref, arrived_ref, *refs):
    cot_refs, out_ref = refs[:X], refs[X]
    grad = jnp.zeros((CH, F), jnp.float32)
    for sx in range(X):
        for sz in range(Z_LO):
            k = (place_ref[0] + X - sx) % X * Z_LO + (place_ref[1] + Z_LO - sz) % Z_LO
            pair = (keep_ref[k] + arrived_ref[k].astype(jnp.float32)).astype(jnp.bfloat16)
            out_ref[k, :NODE] = pair
            grad += lax.dot_general(
                pair, cot_refs[sx][sz], (((0,), (0,)), ((), ())), preferred_element_type=jnp.float32
            )
    grad = grad.astype(jnp.bfloat16)
    per_side = CH // PIECE
    for k in range(ROW_TILES):
        if k < F // PIECE:
            side, part = divmod(k, per_side)
            out_ref[k, NODE:] = grad[part * PIECE : (part + 1) * PIECE, side * CH : (side + 1) * CH]
        else:
            out_ref[k, NODE:] = jnp.zeros((PIECE, CH), jnp.bfloat16)


def pair_stage(place, keep, arrived, cotangents):
    vmem = pl.BlockSpec(memory_space=pltpu.VMEM)
    return pl.pallas_call(
        pair_kernel,
        out_shape=jax.ShapeDtypeStruct((ROW_TILES, NODE + PIECE, CH), jnp.bfloat16),
        in_specs=[pl.BlockSpec(memory_space=pltpu.SMEM)] + [vmem] * (2 + X),
        out_specs=vmem,
        compiler_params=pltpu.CompilerParams(vmem_limit_bytes=16 * 1024 * 1024),
        cost_estimate=pl.CostEstimate(
            flops=2 * ROW_TILES * NODE * CH * F, bytes_accessed=3 * 1024 * 1024, transcendentals=0
        ),
        name="pair_stage",
    )(place, keep, arrived, *cotangents)


def node_kernel(parts_ref, degree_ref, weight_ref, out_ref, grad_ref):
    total = parts_ref[0].astype(jnp.float32)
    for k in range(1, ROW_TILES):
        total += parts_ref[k].astype(jnp.float32)
    grad_ref[...] = total[NODE:]
    aggregated = (
        total[:NODE] * lax.rsqrt(degree_ref[...].astype(jnp.float32))
    ).astype(jnp.bfloat16)
    out_ref[...] = jnp.dot(
        aggregated, weight_ref[...], preferred_element_type=jnp.float32
    ).astype(jnp.bfloat16)


def node_stage(parts, degree, weight):
    vmem = pl.BlockSpec(memory_space=pltpu.VMEM)
    return pl.pallas_call(
        node_kernel,
        out_shape=(
            jax.ShapeDtypeStruct((NODE, F), jnp.bfloat16),
            jax.ShapeDtypeStruct((PIECE, CH), jnp.float32),
        ),
        in_specs=[vmem] * 3,
        out_specs=(vmem, vmem),
        compiler_params=pltpu.CompilerParams(vmem_limit_bytes=8 * 1024 * 1024),
        cost_estimate=pl.CostEstimate(
            flops=2 * NODE * CH * F, bytes_accessed=1024 * 1024, transcendentals=NODE
        ),
        name="node_stage",
    )(parts, degree, weight)


def exchange(parts, axes):
    return lax.all_to_all(parts, axes, 0, 0)


def spread(piece, axes, n):
    return exchange(jnp.broadcast_to(piece[None], (n,) + piece.shape), axes)


def swap_cores(block):
    return lax.ppermute(block, "core", [(0, 1), (1, 0)])


def shifted(block, axis, n, shift):
    return lax.ppermute(block, axis, [(i, (i + shift) % n) for i in range(n)])


def per_device(features, out_degree, in_degree, tile_pos, tile_count, tiles, weight, cotangent):
    core = lax.axis_index("core")
    place = jnp.stack([lax.axis_index("x"), lax.axis_index("zl")])
    scaled = (
        features[0].astype(jnp.float32) * lax.rsqrt(out_degree[0].astype(jnp.float32))[:, None]
    ).astype(jnp.bfloat16)
    over_z = lax.all_gather(scaled, "zh", axis=0)
    copies = jnp.broadcast_to(over_z[None], (Y,) + over_z.shape)
    copies, cotangent, in_degree = lax.optimization_barrier((copies, cotangent, in_degree))
    source = exchange(copies, "y")

    scaled_cot = (
        cotangent[0].astype(jnp.float32)
        * lax.rsqrt(in_degree[0].astype(jnp.float32))[:, None]
    ).astype(jnp.bfloat16)
    over_zl = jnp.stack(
        [scaled_cot] + [shifted(scaled_cot, "zl", Z_LO, s) for s in range(1, Z_LO)]
    )
    cotangents = [over_zl] + [shifted(over_zl, "x", X, s) for s in range(1, X)]
    source, *cotangents = lax.optimization_barrier((source, *cotangents))

    keep, send = tile_product(
        tile_pos[0, 0].T, tile_count[0], core.reshape(1), tiles[0, 0], source
    )
    arrived = swap_cores(send)
    parts = exchange(pair_stage(place, keep, arrived, cotangents), ("x", "zl"))

    output, piece = node_stage(parts, in_degree[0][:, None], weight)

    piece = (piece + swap_cores(piece)).astype(jnp.bfloat16)
    piece = jnp.sum(spread(piece, ROW, N_ROW).astype(jnp.float32), axis=0).astype(jnp.bfloat16)
    pieces = spread(piece, ("x", "zl"), ROW_TILES)
    grad = pieces[: F // PIECE].reshape(F // CH, CH, CH).astype(jnp.float32)
    grad_weight = jnp.concatenate([grad[k] for k in range(F // CH)], axis=1)
    return (output[None], grad_weight)


def solution(mesh):
    fine = Mesh(mesh.devices.reshape(Z_HI, Y, X, Z_LO, CORE), ROW + COL)
    return jax.shard_map(
        per_device,
        mesh=fine,
        in_specs=(
            P(COL, ROW, None),
            P(COL, ROW),
            P(ROW, COL),
            P(ROW, COL, None, None),
            P(ROW, COL),
            P(ROW, COL, None, None, None),
            P(),
            P(ROW, COL, None),
        ),
        out_specs=(P(ROW, COL, None), P()),
        check_vma=False,
    )
```

```python
import jax
import jax.numpy as jnp
from jax import lax
from jax.experimental import pallas as pl
from jax.experimental.pallas import tpu as pltpu
from jax.sharding import Mesh, PartitionSpec as P

Z_HI, Y, X, Z_LO, CORE = 4, 8, 4, 3, 2
ROW = ("zh", "y")
COL = ("x", "zl", "core")
NODE = 128
TILE = 256
CH = 128
F = 256
ROW_TILES = X * Z_LO
COL_TILES = Z_HI * Y * NODE // TILE
N_ROW = Z_HI * Y
PIECE = 32
UNROLL = 4


def tile_kernel(
    pos_ref, count_ref, core_ref, tiles_ref, source_ref, keep_ref, send_ref, acc_ref, held_ref, sems
):
    count = count_ref[0]
    core = core_ref[0]
    chunks = tiles_ref.shape[0] // UNROLL

    def fetch(k):
        slots = pl.ds(k * UNROLL, UNROLL)
        return pltpu.make_async_copy(tiles_ref.at[slots], held_ref.at[slots], sems.at[k])

    for k in range(chunks):
        fetch(k).start()
    acc_ref[...] = jnp.zeros_like(acc_ref)

    def chunk(k, carry):
        fetch(k).wait()

        @pl.when(k * UNROLL < count)
        def _():
            products = []
            for u in range(UNROLL):
                s = k * UNROLL + u
                j = pos_ref[s] % COL_TILES
                picked = source_ref[pl.ds(2 * (j % (Y // 2)), 2), j // (Y // 2)].reshape(TILE, CH)
                picked = jnp.where(s < count, picked, jnp.zeros_like(picked))
                products.append(jnp.dot(held_ref[s], picked, preferred_element_type=jnp.float32))
            for u in range(UNROLL):
                i = pos_ref[k * UNROLL + u] // COL_TILES
                acc_ref[i] += products[u].reshape(CORE, NODE, CH)

        return carry

    lax.fori_loop(0, chunks, chunk, 0)
    keep_ref[...] = acc_ref[:, core]
    send_ref[...] = acc_ref[:, 1 - core].astype(jnp.bfloat16)


def tile_product(positions, count, core, tiles, source):
    smem = pl.BlockSpec(memory_space=pltpu.SMEM)
    vmem = pl.BlockSpec(memory_space=pltpu.VMEM)
    return pl.pallas_call(
        tile_kernel,
        out_shape=(
            jax.ShapeDtypeStruct((ROW_TILES, NODE, CH), jnp.float32),
            jax.ShapeDtypeStruct((ROW_TILES, NODE, CH), jnp.bfloat16),
        ),
        in_specs=[smem, smem, smem, pl.BlockSpec(memory_space=pltpu.HBM), vmem],
        out_specs=(vmem, vmem),
        scratch_shapes=[
            pltpu.VMEM((ROW_TILES, CORE, NODE, CH), jnp.float32),
            pltpu.VMEM(tiles.shape, tiles.dtype),
            pltpu.SemaphoreType.DMA((tiles.shape[0] // UNROLL,)),
        ],
        compiler_params=pltpu.CompilerParams(vmem_limit_bytes=50 * 1024 * 1024),
        cost_estimate=pl.CostEstimate(
            flops=2 * 32 * TILE * TILE * CH, bytes_accessed=8 * 1024 * 1024, transcendentals=0
        ),
        name="tile_product",
    )(positions, count, core, tiles, source)


def pair_kernel(place_ref, keep_ref, arrived_ref, *refs):
    cot_refs, out_ref = refs[:X], refs[X]
    grad = jnp.zeros((CH, F), jnp.float32)
    for sx in range(X):
        for sz in range(Z_LO):
            k = (place_ref[0] + X - sx) % X * Z_LO + (place_ref[1] + Z_LO - sz) % Z_LO
            pair = (keep_ref[k] + arrived_ref[k].astype(jnp.float32)).astype(jnp.bfloat16)
            out_ref[k, :NODE] = pair
            grad += lax.dot_general(
                pair, cot_refs[sx][sz], (((0,), (0,)), ((), ())), preferred_element_type=jnp.float32
            )
    grad = grad.astype(jnp.bfloat16)
    per_side = CH // PIECE
    for k in range(ROW_TILES):
        if k < F // PIECE:
            side, part = divmod(k, per_side)
            out_ref[k, NODE:] = grad[part * PIECE : (part + 1) * PIECE, side * CH : (side + 1) * CH]
        else:
            out_ref[k, NODE:] = jnp.zeros((PIECE, CH), jnp.bfloat16)


def pair_stage(place, keep, arrived, cotangents):
    vmem = pl.BlockSpec(memory_space=pltpu.VMEM)
    return pl.pallas_call(
        pair_kernel,
        out_shape=jax.ShapeDtypeStruct((ROW_TILES, NODE + PIECE, CH), jnp.bfloat16),
        in_specs=[pl.BlockSpec(memory_space=pltpu.SMEM)] + [vmem] * (2 + X),
        out_specs=vmem,
        compiler_params=pltpu.CompilerParams(vmem_limit_bytes=16 * 1024 * 1024),
        cost_estimate=pl.CostEstimate(
            flops=2 * ROW_TILES * NODE * CH * F, bytes_accessed=3 * 1024 * 1024, transcendentals=0
        ),
        name="pair_stage",
    )(place, keep, arrived, *cotangents)


def node_kernel(parts_ref, degree_ref, weight_ref, out_ref, grad_ref):
    total = parts_ref[0].astype(jnp.float32)
    for k in range(1, ROW_TILES):
        total += parts_ref[k].astype(jnp.float32)
    grad_ref[...] = total[NODE:]
    aggregated = (
        total[:NODE] * lax.rsqrt(degree_ref[...].astype(jnp.float32))
    ).astype(jnp.bfloat16)
    out_ref[...] = jnp.dot(
        aggregated, weight_ref[...], preferred_element_type=jnp.float32
    ).astype(jnp.bfloat16)


def node_stage(parts, degree, weight):
    vmem = pl.BlockSpec(memory_space=pltpu.VMEM)
    return pl.pallas_call(
        node_kernel,
        out_shape=(
            jax.ShapeDtypeStruct((NODE, F), jnp.bfloat16),
            jax.ShapeDtypeStruct((PIECE, CH), jnp.float32),
        ),
        in_specs=[vmem] * 3,
        out_specs=(vmem, vmem),
        compiler_params=pltpu.CompilerParams(vmem_limit_bytes=8 * 1024 * 1024),
        cost_estimate=pl.CostEstimate(
            flops=2 * NODE * CH * F, bytes_accessed=1024 * 1024, transcendentals=NODE
        ),
        name="node_stage",
    )(parts, degree, weight)


def exchange(parts, axes):
    return lax.all_to_all(parts, axes, 0, 0)


def spread(piece, axes, n):
    return exchange(jnp.broadcast_to(piece[None], (n,) + piece.shape), axes)


def swap_cores(block):
    return lax.ppermute(block, "core", [(0, 1), (1, 0)])


def shifted(block, axis, n, shift):
    return lax.ppermute(block, axis, [(i, (i + shift) % n) for i in range(n)])


def per_device(features, out_degree, in_degree, tile_pos, tile_count, tiles, weight, cotangent):
    core = lax.axis_index("core")
    place = jnp.stack([lax.axis_index("x"), lax.axis_index("zl")])
    scaled = (
        features[0].astype(jnp.float32) * lax.rsqrt(out_degree[0].astype(jnp.float32))[:, None]
    ).astype(jnp.bfloat16)
    over_z = lax.all_gather(scaled, "zh", axis=0)
    copies = jnp.broadcast_to(over_z[None], (Y,) + over_z.shape)
    copies, cotangent, in_degree, tile_pos = lax.optimization_barrier(
        (copies, cotangent, in_degree, tile_pos)
    )
    source = exchange(copies, "y")

    scaled_cot = (
        cotangent.astype(jnp.float32) * lax.rsqrt(in_degree.astype(jnp.float32))[:, :, None]
    ).astype(jnp.bfloat16)
    over_zl = jnp.concatenate(
        [scaled_cot] + [shifted(scaled_cot, "zl", Z_LO, s) for s in range(1, Z_LO)]
    )
    cotangents = [over_zl] + [shifted(over_zl, "x", X, s) for s in range(1, X)]
    places = tile_pos[0, 0, :, 0] * COL_TILES + tile_pos[0, 0, :, 1]
    source, places, *cotangents = lax.optimization_barrier((source, places, *cotangents))

    keep, send = tile_product(
        places, tile_count[0], core.reshape(1), tiles[0, 0], source
    )
    arrived = swap_cores(send)
    parts = exchange(pair_stage(place, keep, arrived, cotangents), ("x", "zl"))

    output, piece = node_stage(parts, in_degree[0][:, None], weight)

    halves = piece.reshape(CORE, PIECE // CORE, CH)
    own = lax.dynamic_index_in_dim(halves, core, 0, keepdims=False)
    other = lax.dynamic_index_in_dim(halves, 1 - core, 0, keepdims=False)
    piece = (own + swap_cores(other)).astype(jnp.bfloat16)
    piece = jnp.sum(spread(piece, ROW, N_ROW).astype(jnp.float32), axis=0).astype(jnp.bfloat16)
    pieces = spread(piece, COL, CORE * ROW_TILES)
    grad = pieces[: CORE * F // PIECE].reshape(F // CH, CH, CH).astype(jnp.float32)
    grad_weight = jnp.concatenate([grad[k] for k in range(F // CH)], axis=1)
    return (output[None], grad_weight)


def solution(mesh):
    fine = Mesh(mesh.devices.reshape(Z_HI, Y, X, Z_LO, CORE), ROW + COL)
    return jax.shard_map(
        per_device,
        mesh=fine,
        in_specs=(
            P(COL, ROW, None),
            P(COL, ROW),
            P(ROW, COL),
            P(ROW, COL, None, None),
            P(ROW, COL),
            P(ROW, COL, None, None, None),
            P(),
            P(ROW, COL, None),
        ),
        out_specs=(P(ROW, COL, None), P()),
        check_vma=False,
    )
```

```python
import jax
import jax.numpy as jnp
from jax import lax
from jax.experimental import pallas as pl
from jax.experimental.pallas import tpu as pltpu
from jax.sharding import Mesh, PartitionSpec as P

Z_HI, Y, X, Z_LO, CORE = 4, 8, 4, 3, 2
ROW = ("zh", "y")
COL = ("x", "zl", "core")
NODE = 128
TILE = 256
CH = 128
F = 256
ROW_TILES = X * Z_LO
COL_TILES = Z_HI * Y * NODE // TILE
N_ROW = Z_HI * Y
PIECE = 32
UNROLL = 8


def scale_kernel(features_ref, degree_ref, copies_ref):
    factor = lax.rsqrt(degree_ref[...].astype(jnp.float32))
    factor = jnp.broadcast_to(factor, (NODE, NODE)).T
    scaled = (features_ref[...].astype(jnp.float32) * factor).astype(jnp.bfloat16)
    for k in range(Z_HI):
        copies_ref[k] = scaled


def scaled_copies(features, degree):
    vmem = pl.BlockSpec(memory_space=pltpu.VMEM)
    return pl.pallas_call(
        scale_kernel,
        out_shape=jax.ShapeDtypeStruct((Z_HI, NODE, CH), jnp.bfloat16),
        in_specs=[vmem, vmem],
        out_specs=vmem,
        compiler_params=pltpu.CompilerParams(vmem_limit_bytes=8 * 1024 * 1024),
        cost_estimate=pl.CostEstimate(
            flops=NODE * CH, bytes_accessed=256 * 1024, transcendentals=NODE
        ),
        name="scaled_copies",
    )(features, degree)


def tile_kernel(
    pos_ref, count_ref, core_ref, tiles_ref, source_ref, keep_ref, send_ref, acc_ref, held_ref, sems
):
    count = count_ref[0]
    core = core_ref[0]
    chunks = tiles_ref.shape[0] // UNROLL

    def fetch(k):
        slots = pl.ds(k * UNROLL, UNROLL)
        return pltpu.make_async_copy(tiles_ref.at[slots], held_ref.at[slots], sems.at[k])

    for k in range(chunks):
        fetch(k).start()
    acc_ref[...] = jnp.zeros_like(acc_ref)

    def chunk(k, carry):
        fetch(k).wait()

        @pl.when(k * UNROLL < count)
        def _():
            for u in range(UNROLL):
                s = k * UNROLL + u
                i, j = pos_ref[s] // COL_TILES, pos_ref[s] % COL_TILES
                picked = source_ref[pl.ds(2 * (j % (Y // 2)), 2), j // (Y // 2)].reshape(TILE, CH)
                picked = jnp.where(s < count, picked, jnp.zeros_like(picked))
                product = jnp.dot(held_ref[s], picked, preferred_element_type=jnp.float32)
                acc_ref[i] += product.reshape(CORE, NODE, CH)

        return carry

    lax.fori_loop(0, chunks, chunk, 0)
    keep_ref[...] = acc_ref[:, core]
    send_ref[...] = acc_ref[:, 1 - core].astype(jnp.bfloat16)


def tile_product(positions, count, core, tiles, source):
    smem = pl.BlockSpec(memory_space=pltpu.SMEM)
    vmem = pl.BlockSpec(memory_space=pltpu.VMEM)
    return pl.pallas_call(
        tile_kernel,
        out_shape=(
            jax.ShapeDtypeStruct((ROW_TILES, NODE, CH), jnp.float32),
            jax.ShapeDtypeStruct((ROW_TILES, NODE, CH), jnp.bfloat16),
        ),
        in_specs=[smem, smem, smem, pl.BlockSpec(memory_space=pltpu.HBM), vmem],
        out_specs=(vmem, vmem),
        scratch_shapes=[
            pltpu.VMEM((ROW_TILES, CORE, NODE, CH), jnp.float32),
            pltpu.VMEM(tiles.shape, tiles.dtype),
            pltpu.SemaphoreType.DMA((tiles.shape[0] // UNROLL,)),
        ],
        compiler_params=pltpu.CompilerParams(vmem_limit_bytes=50 * 1024 * 1024),
        cost_estimate=pl.CostEstimate(
            flops=2 * 32 * TILE * TILE * CH, bytes_accessed=8 * 1024 * 1024, transcendentals=0
        ),
        name="tile_product",
    )(positions, count, core, tiles, source)


def pair_kernel(place_ref, keep_ref, arrived_ref, *refs):
    cot_refs, out_ref = refs[:X], refs[X]
    grad = jnp.zeros((CH, F), jnp.float32)
    for sx in range(X):
        for sz in range(Z_LO):
            k = (place_ref[0] + X - sx) % X * Z_LO + (place_ref[1] + Z_LO - sz) % Z_LO
            pair = (keep_ref[k] + arrived_ref[k].astype(jnp.float32)).astype(jnp.bfloat16)
            out_ref[k % Z_LO * X + k // Z_LO, :NODE] = pair
            grad += lax.dot_general(
                pair, cot_refs[sx][sz], (((0,), (0,)), ((), ())), preferred_element_type=jnp.float32
            )
    grad = grad.astype(jnp.bfloat16)
    per_side = CH // PIECE
    for k in range(ROW_TILES):
        if k < F // PIECE:
            side, part = divmod(k, per_side)
            out_ref[k, NODE:] = grad[part * PIECE : (part + 1) * PIECE, side * CH : (side + 1) * CH]
        else:
            out_ref[k, NODE:] = jnp.zeros((PIECE, CH), jnp.bfloat16)


def pair_stage(place, keep, arrived, cotangents):
    vmem = pl.BlockSpec(memory_space=pltpu.VMEM)
    return pl.pallas_call(
        pair_kernel,
        out_shape=jax.ShapeDtypeStruct((ROW_TILES, NODE + PIECE, CH), jnp.bfloat16),
        in_specs=[pl.BlockSpec(memory_space=pltpu.SMEM)] + [vmem] * (2 + X),
        out_specs=vmem,
        compiler_params=pltpu.CompilerParams(vmem_limit_bytes=16 * 1024 * 1024),
        cost_estimate=pl.CostEstimate(
            flops=2 * ROW_TILES * NODE * CH * F, bytes_accessed=3 * 1024 * 1024, transcendentals=0
        ),
        name="pair_stage",
    )(place, keep, arrived, *cotangents)


def node_kernel(parts_ref, degree_ref, weight_ref, out_ref, grad_ref):
    total = parts_ref[0].astype(jnp.float32)
    for k in range(1, ROW_TILES):
        total += parts_ref[k].astype(jnp.float32)
    grad_ref[...] = total[NODE:]
    aggregated = (
        total[:NODE] * lax.rsqrt(degree_ref[...].astype(jnp.float32))
    ).astype(jnp.bfloat16)
    out_ref[...] = jnp.dot(
        aggregated, weight_ref[...], preferred_element_type=jnp.float32
    ).astype(jnp.bfloat16)


def node_stage(parts, degree, weight):
    vmem = pl.BlockSpec(memory_space=pltpu.VMEM)
    return pl.pallas_call(
        node_kernel,
        out_shape=(
            jax.ShapeDtypeStruct((NODE, F), jnp.bfloat16),
            jax.ShapeDtypeStruct((PIECE, CH), jnp.float32),
        ),
        in_specs=[vmem] * 3,
        out_specs=(vmem, vmem),
        compiler_params=pltpu.CompilerParams(vmem_limit_bytes=8 * 1024 * 1024),
        cost_estimate=pl.CostEstimate(
            flops=2 * NODE * CH * F, bytes_accessed=1024 * 1024, transcendentals=NODE
        ),
        name="node_stage",
    )(parts, degree, weight)


def exchange(parts, axes):
    return lax.all_to_all(parts, axes, 0, 0)


def spread(piece, axes, n):
    return exchange(jnp.broadcast_to(piece[None], (n,) + piece.shape), axes)


def swap_cores(block):
    return lax.ppermute(block, "core", [(0, 1), (1, 0)])


def shifted(block, axis, n, shift):
    return lax.ppermute(block, axis, [(i, (i + shift) % n) for i in range(n)])


def per_device(features, out_degree, in_degree, tile_pos, tile_count, tiles, weight, cotangent):
    core = lax.axis_index("core")
    place = jnp.stack([lax.axis_index("x"), lax.axis_index("zl")])
    over_z = exchange(scaled_copies(features[0], out_degree), "zh")
    copies = jnp.broadcast_to(over_z[None], (Y,) + over_z.shape)
    copies, cotangent, in_degree, tile_pos = lax.optimization_barrier(
        (copies, cotangent, in_degree, tile_pos)
    )
    source = exchange(copies, "y")

    scaled_cot = (
        cotangent.astype(jnp.float32) * lax.rsqrt(in_degree.astype(jnp.float32))[:, :, None]
    ).astype(jnp.bfloat16)
    over_zl = jnp.concatenate(
        [scaled_cot] + [shifted(scaled_cot, "zl", Z_LO, s) for s in range(1, Z_LO)]
    )
    cotangents = [over_zl] + [shifted(over_zl, "x", X, s) for s in range(1, X)]
    places = tile_pos[0, 0, :, 0] * COL_TILES + tile_pos[0, 0, :, 1]
    source, places, *cotangents = lax.optimization_barrier((source, places, *cotangents))

    keep, send = tile_product(
        places, tile_count[0], core.reshape(1), tiles[0, 0], source
    )
    arrived = swap_cores(send)
    parts = exchange(pair_stage(place, keep, arrived, cotangents), ("zl", "x"))

    output, piece = node_stage(parts, in_degree[0][:, None], weight)

    halves = piece.reshape(CORE, PIECE // CORE, CH)
    own = lax.dynamic_index_in_dim(halves, core, 0, keepdims=False)
    other = lax.dynamic_index_in_dim(halves, 1 - core, 0, keepdims=False)
    piece = (own + swap_cores(other)).astype(jnp.bfloat16)
    piece = jnp.sum(spread(piece, ROW, N_ROW).astype(jnp.float32), axis=0).astype(jnp.bfloat16)
    pieces = spread(piece, ("zl", "x", "core"), CORE * ROW_TILES)
    grad = pieces[: CORE * F // PIECE].reshape(F // CH, CH, CH).astype(jnp.float32)
    grad_weight = jnp.concatenate([grad[k] for k in range(F // CH)], axis=1)
    return (output[None], grad_weight)


def solution(mesh):
    fine = Mesh(mesh.devices.reshape(Z_HI, Y, X, Z_LO, CORE), ROW + COL)
    return jax.shard_map(
        per_device,
        mesh=fine,
        in_specs=(
            P(COL, ROW, None),
            P(COL, ROW),
            P(ROW, COL),
            P(ROW, COL, None, None),
            P(ROW, COL),
            P(ROW, COL, None, None, None),
            P(),
            P(ROW, COL, None),
        ),
        out_specs=(P(ROW, COL, None), P()),
        check_vma=False,
    )
```

```python
import jax
import jax.numpy as jnp
from jax import lax
from jax.experimental import pallas as pl
from jax.experimental.pallas import tpu as pltpu
from jax.sharding import Mesh, PartitionSpec as P

Z_HI, Y, X, Z_LO, CORE = 4, 8, 4, 3, 2
ROW = ("zh", "y")
COL = ("x", "zl", "core")
NODE = 128
TILE = 256
CH = 128
F = 256
ROW_TILES = X * Z_LO
COL_TILES = Z_HI * Y * NODE // TILE
N_ROW = Z_HI * Y
PIECE = 32
UNROLL = 8


def scale_kernel(features_ref, degree_ref, copies_ref):
    factor = lax.rsqrt(degree_ref[...].astype(jnp.float32))
    factor = jnp.broadcast_to(factor, (NODE, NODE)).T
    scaled = (features_ref[...].astype(jnp.float32) * factor).astype(jnp.bfloat16)
    for k in range(Z_HI):
        copies_ref[k] = scaled


def scaled_copies(features, degree):
    vmem = pl.BlockSpec(memory_space=pltpu.VMEM)
    return pl.pallas_call(
        scale_kernel,
        out_shape=jax.ShapeDtypeStruct((Z_HI, NODE, CH), jnp.bfloat16),
        in_specs=[vmem, vmem],
        out_specs=vmem,
        compiler_params=pltpu.CompilerParams(vmem_limit_bytes=8 * 1024 * 1024),
        cost_estimate=pl.CostEstimate(
            flops=NODE * CH, bytes_accessed=256 * 1024, transcendentals=NODE
        ),
        name="scaled_copies",
    )(features, degree)


def tile_kernel(
    pos_ref, count_ref, core_ref, tiles_ref, source_ref, keep_ref, send_ref, acc_ref, held_ref, sems
):
    count = count_ref[0]
    core = core_ref[0]
    chunks = tiles_ref.shape[0] // UNROLL

    def fetch(k):
        slots = pl.ds(k * UNROLL, UNROLL)
        return pltpu.make_async_copy(tiles_ref.at[slots], held_ref.at[slots], sems.at[k])

    for k in range(chunks):
        fetch(k).start()
    acc_ref[...] = jnp.zeros_like(acc_ref)

    def chunk(k, carry):
        fetch(k).wait()

        @pl.when(k * UNROLL < count)
        def _():
            for u in range(UNROLL):
                s = k * UNROLL + u
                i, j = pos_ref[s] // COL_TILES, pos_ref[s] % COL_TILES
                picked = source_ref[pl.ds(2 * (j % (Y // 2)), 2), j // (Y // 2)].reshape(TILE, CH)
                picked = jnp.where(s < count, picked, jnp.zeros_like(picked))
                product = jnp.dot(held_ref[s], picked, preferred_element_type=jnp.float32)
                acc_ref[i] += product.reshape(CORE, NODE, CH)

        return carry

    lax.fori_loop(0, chunks, chunk, 0)
    keep_ref[...] = acc_ref[:, core]
    send_ref[...] = acc_ref[:, 1 - core].astype(jnp.bfloat16)


def tile_product(positions, count, core, tiles, source):
    smem = pl.BlockSpec(memory_space=pltpu.SMEM)
    vmem = pl.BlockSpec(memory_space=pltpu.VMEM)
    return pl.pallas_call(
        tile_kernel,
        out_shape=(
            jax.ShapeDtypeStruct((ROW_TILES, NODE, CH), jnp.float32),
            jax.ShapeDtypeStruct((ROW_TILES, NODE, CH), jnp.bfloat16),
        ),
        in_specs=[smem, smem, smem, pl.BlockSpec(memory_space=pltpu.HBM), vmem],
        out_specs=(vmem, vmem),
        scratch_shapes=[
            pltpu.VMEM((ROW_TILES, CORE, NODE, CH), jnp.float32),
            pltpu.VMEM(tiles.shape, tiles.dtype),
            pltpu.SemaphoreType.DMA((tiles.shape[0] // UNROLL,)),
        ],
        compiler_params=pltpu.CompilerParams(vmem_limit_bytes=50 * 1024 * 1024),
        cost_estimate=pl.CostEstimate(
            flops=2 * 32 * TILE * TILE * CH, bytes_accessed=8 * 1024 * 1024, transcendentals=0
        ),
        name="tile_product",
    )(positions, count, core, tiles, source)


def pair_kernel(place_ref, keep_ref, arrived_ref, *refs):
    cot_refs, out_ref = refs[:X], refs[X]
    grad = jnp.zeros((CH, F), jnp.float32)
    for sx in range(X):
        for sz in range(Z_LO):
            k = (place_ref[0] + X - sx) % X * Z_LO + (place_ref[1] + Z_LO - sz) % Z_LO
            pair = (keep_ref[k] + arrived_ref[k].astype(jnp.float32)).astype(jnp.bfloat16)
            out_ref[k % Z_LO * X + k // Z_LO, :NODE] = pair
            grad += lax.dot_general(
                pair, cot_refs[sx][sz], (((0,), (0,)), ((), ())), preferred_element_type=jnp.float32
            )
    grad = grad.astype(jnp.bfloat16)
    per_side = CH // PIECE
    for k in range(ROW_TILES):
        if k < F // PIECE:
            side, part = divmod(k, per_side)
            out_ref[k, NODE:] = grad[part * PIECE : (part + 1) * PIECE, side * CH : (side + 1) * CH]
        else:
            out_ref[k, NODE:] = jnp.zeros((PIECE, CH), jnp.bfloat16)


def pair_stage(place, keep, arrived, cotangents):
    vmem = pl.BlockSpec(memory_space=pltpu.VMEM)
    return pl.pallas_call(
        pair_kernel,
        out_shape=jax.ShapeDtypeStruct((ROW_TILES, NODE + PIECE, CH), jnp.bfloat16),
        in_specs=[pl.BlockSpec(memory_space=pltpu.SMEM)] + [vmem] * (2 + X),
        out_specs=vmem,
        compiler_params=pltpu.CompilerParams(vmem_limit_bytes=16 * 1024 * 1024),
        cost_estimate=pl.CostEstimate(
            flops=2 * ROW_TILES * NODE * CH * F, bytes_accessed=3 * 1024 * 1024, transcendentals=0
        ),
        name="pair_stage",
    )(place, keep, arrived, *cotangents)


def node_kernel(parts_ref, degree_ref, weight_ref, out_ref, grad_ref):
    total = parts_ref[0].astype(jnp.float32)
    for k in range(1, ROW_TILES):
        total += parts_ref[k].astype(jnp.float32)
    grad_ref[...] = total[NODE:]
    aggregated = (
        total[:NODE] * lax.rsqrt(degree_ref[...].astype(jnp.float32))
    ).astype(jnp.bfloat16)
    out_ref[...] = jnp.dot(
        aggregated, weight_ref[...], preferred_element_type=jnp.float32
    ).astype(jnp.bfloat16)


def node_stage(parts, degree, weight):
    vmem = pl.BlockSpec(memory_space=pltpu.VMEM)
    return pl.pallas_call(
        node_kernel,
        out_shape=(
            jax.ShapeDtypeStruct((NODE, F), jnp.bfloat16),
            jax.ShapeDtypeStruct((PIECE, CH), jnp.float32),
        ),
        in_specs=[vmem] * 3,
        out_specs=(vmem, vmem),
        compiler_params=pltpu.CompilerParams(vmem_limit_bytes=8 * 1024 * 1024),
        cost_estimate=pl.CostEstimate(
            flops=2 * NODE * CH * F, bytes_accessed=1024 * 1024, transcendentals=NODE
        ),
        name="node_stage",
    )(parts, degree, weight)


def exchange(parts, axes):
    return lax.all_to_all(parts, axes, 0, 0)


def spread(piece, axes, n):
    return exchange(jnp.broadcast_to(piece[None], (n,) + piece.shape), axes)


def swap_cores(block):
    return lax.ppermute(block, "core", [(0, 1), (1, 0)])


def shifted(block, axis, n, shift):
    return lax.ppermute(block, axis, [(i, (i + shift) % n) for i in range(n)])


def per_device(features, out_degree, in_degree, tile_pos, tile_count, tiles, weight, cotangent):
    core = lax.axis_index("core")
    place = jnp.stack([lax.axis_index("x"), lax.axis_index("zl")])
    over_z = exchange(scaled_copies(features[0], out_degree), "zh")
    copies = jnp.broadcast_to(over_z[None], (Y,) + over_z.shape)
    copies, cotangent, in_degree, tile_pos = lax.optimization_barrier(
        (copies, cotangent, in_degree, tile_pos)
    )
    source = exchange(copies, "y")

    scaled_cot = (
        cotangent.astype(jnp.float32) * lax.rsqrt(in_degree.astype(jnp.float32))[:, :, None]
    ).astype(jnp.bfloat16)
    over_zl = jnp.concatenate(
        [scaled_cot] + [shifted(scaled_cot, "zl", Z_LO, s) for s in range(1, Z_LO)]
    )
    cotangents = [over_zl] + [shifted(over_zl, "x", X, s) for s in range(1, X)]
    places = tile_pos[0, 0, :, 0] * COL_TILES + tile_pos[0, 0, :, 1]
    source, places, *cotangents = lax.optimization_barrier((source, places, *cotangents))

    keep, send = tile_product(
        places, tile_count[0], core.reshape(1), tiles[0, 0], source
    )
    arrived = swap_cores(send)
    parts = exchange(pair_stage(place, keep, arrived, cotangents), ("zl", "x"))

    output, piece = node_stage(parts, in_degree[0][:, None], weight)

    halves = jnp.broadcast_to(
        piece.astype(jnp.bfloat16).reshape(1, CORE, PIECE // CORE, CH),
        (Y, CORE, PIECE // CORE, CH),
    ).reshape(Y * CORE, PIECE // CORE, CH)
    piece = jnp.sum(exchange(halves, ("y", "core")).astype(jnp.float32), axis=0)
    piece = lax.psum(piece, "zh").astype(jnp.bfloat16)
    pieces = spread(piece, ("zl", "x", "core"), CORE * ROW_TILES)
    grad = pieces[: CORE * F // PIECE].reshape(F // CH, CH, CH).astype(jnp.float32)
    grad_weight = jnp.concatenate([grad[k] for k in range(F // CH)], axis=1)
    return (output[None], grad_weight)


def solution(mesh):
    fine = Mesh(mesh.devices.reshape(Z_HI, Y, X, Z_LO, CORE), ROW + COL)
    return jax.shard_map(
        per_device,
        mesh=fine,
        in_specs=(
            P(COL, ROW, None),
            P(COL, ROW),
            P(ROW, COL),
            P(ROW, COL, None, None),
            P(ROW, COL),
            P(ROW, COL, None, None, None),
            P(),
            P(ROW, COL, None),
        ),
        out_specs=(P(ROW, COL, None), P()),
        check_vma=False,
    )
```

```python
import jax
import jax.numpy as jnp
from jax import lax
from jax.experimental import pallas as pl
from jax.experimental.pallas import tpu as pltpu
from jax.sharding import Mesh, PartitionSpec as P

Z_HI, Y, X, Z_LO, CORE = 4, 8, 4, 3, 2
ROW = ("zh", "y")
COL = ("x", "zl", "core")
NODE = 128
TILE = 256
CH = 128
F = 256
ROW_TILES = X * Z_LO
COL_TILES = Z_HI * Y * NODE // TILE
N_ROW = Z_HI * Y
PIECE = 32
UNROLL = 8


def scale_kernel(features_ref, degree_ref, copies_ref):
    factor = lax.rsqrt(degree_ref[...].astype(jnp.float32))
    factor = jnp.broadcast_to(factor, (NODE, NODE)).T
    scaled = (features_ref[...].astype(jnp.float32) * factor).astype(jnp.bfloat16)
    for k in range(Z_HI):
        copies_ref[k] = scaled


def scaled_copies(features, degree):
    vmem = pl.BlockSpec(memory_space=pltpu.VMEM)
    return pl.pallas_call(
        scale_kernel,
        out_shape=jax.ShapeDtypeStruct((Z_HI, NODE, CH), jnp.bfloat16),
        in_specs=[vmem, vmem],
        out_specs=vmem,
        compiler_params=pltpu.CompilerParams(vmem_limit_bytes=8 * 1024 * 1024),
        cost_estimate=pl.CostEstimate(
            flops=NODE * CH, bytes_accessed=256 * 1024, transcendentals=NODE
        ),
        name="scaled_copies",
    )(features, degree)


def tile_kernel(
    pos_ref, count_ref, core_ref, tiles_ref, source_ref, keep_ref, send_ref, acc_ref, held_ref, sems
):
    count = count_ref[0]
    core = core_ref[0]
    chunks = tiles_ref.shape[0] // UNROLL

    def fetch(k):
        slots = pl.ds(k * UNROLL, UNROLL)
        return pltpu.make_async_copy(tiles_ref.at[slots], held_ref.at[slots], sems.at[k])

    for k in range(chunks):
        fetch(k).start()
    acc_ref[...] = jnp.zeros_like(acc_ref)

    def chunk(k, carry):
        fetch(k).wait()

        @pl.when(k * UNROLL < count)
        def _():
            for u in range(UNROLL):
                s = k * UNROLL + u
                i, j = pos_ref[s] // COL_TILES, pos_ref[s] % COL_TILES
                picked = source_ref[pl.ds(2 * (j % (Y // 2)), 2), j // (Y // 2)].reshape(TILE, CH)
                picked = jnp.where(s < count, picked, jnp.zeros_like(picked))
                product = jnp.dot(held_ref[s], picked, preferred_element_type=jnp.float32)
                acc_ref[i] += product.reshape(CORE, NODE, CH)

        return carry

    lax.fori_loop(0, chunks, chunk, 0)
    keep_ref[...] = acc_ref[:, core]
    send_ref[...] = acc_ref[:, 1 - core].astype(jnp.bfloat16)


def tile_product(positions, count, core, tiles, source):
    smem = pl.BlockSpec(memory_space=pltpu.SMEM)
    vmem = pl.BlockSpec(memory_space=pltpu.VMEM)
    return pl.pallas_call(
        tile_kernel,
        out_shape=(
            jax.ShapeDtypeStruct((ROW_TILES, NODE, CH), jnp.float32),
            jax.ShapeDtypeStruct((ROW_TILES, NODE, CH), jnp.bfloat16),
        ),
        in_specs=[smem, smem, smem, pl.BlockSpec(memory_space=pltpu.HBM), vmem],
        out_specs=(vmem, vmem),
        scratch_shapes=[
            pltpu.VMEM((ROW_TILES, CORE, NODE, CH), jnp.float32),
            pltpu.VMEM(tiles.shape, tiles.dtype),
            pltpu.SemaphoreType.DMA((tiles.shape[0] // UNROLL,)),
        ],
        compiler_params=pltpu.CompilerParams(vmem_limit_bytes=50 * 1024 * 1024),
        cost_estimate=pl.CostEstimate(
            flops=2 * 32 * TILE * TILE * CH, bytes_accessed=8 * 1024 * 1024, transcendentals=0
        ),
        name="tile_product",
    )(positions, count, core, tiles, source)


def pair_kernel(place_ref, keep_ref, arrived_ref, *refs):
    cot_refs, out_ref = refs[:X], refs[X]
    grad = jnp.zeros((CH, F), jnp.float32)
    for sx in range(X):
        for sz in range(Z_LO):
            k = (place_ref[0] + X - sx) % X * Z_LO + (place_ref[1] + Z_LO - sz) % Z_LO
            pair = (keep_ref[k] + arrived_ref[k].astype(jnp.float32)).astype(jnp.bfloat16)
            out_ref[k % Z_LO * X + k // Z_LO, :NODE] = pair
            grad += lax.dot_general(
                pair, cot_refs[sx][sz], (((0,), (0,)), ((), ())), preferred_element_type=jnp.float32
            )
    grad = grad.astype(jnp.bfloat16)
    per_side = CH // PIECE
    for k in range(ROW_TILES):
        if k < F // PIECE:
            side, part = divmod(k, per_side)
            out_ref[k, NODE:] = grad[part * PIECE : (part + 1) * PIECE, side * CH : (side + 1) * CH]
        else:
            out_ref[k, NODE:] = jnp.zeros((PIECE, CH), jnp.bfloat16)


def pair_stage(place, keep, arrived, cotangents):
    vmem = pl.BlockSpec(memory_space=pltpu.VMEM)
    return pl.pallas_call(
        pair_kernel,
        out_shape=jax.ShapeDtypeStruct((ROW_TILES, NODE + PIECE, CH), jnp.bfloat16),
        in_specs=[pl.BlockSpec(memory_space=pltpu.SMEM)] + [vmem] * (2 + X),
        out_specs=vmem,
        compiler_params=pltpu.CompilerParams(vmem_limit_bytes=16 * 1024 * 1024),
        cost_estimate=pl.CostEstimate(
            flops=2 * ROW_TILES * NODE * CH * F, bytes_accessed=3 * 1024 * 1024, transcendentals=0
        ),
        name="pair_stage",
    )(place, keep, arrived, *cotangents)


def node_kernel(parts_ref, degree_ref, weight_ref, out_ref, grad_ref):
    total = parts_ref[0].astype(jnp.float32)
    for k in range(1, ROW_TILES):
        total += parts_ref[k].astype(jnp.float32)
    grad_ref[...] = total[NODE:]
    aggregated = (
        total[:NODE] * lax.rsqrt(degree_ref[...].astype(jnp.float32))
    ).astype(jnp.bfloat16)
    out_ref[...] = jnp.dot(
        aggregated, weight_ref[...], preferred_element_type=jnp.float32
    ).astype(jnp.bfloat16)


def node_stage(parts, degree, weight):
    vmem = pl.BlockSpec(memory_space=pltpu.VMEM)
    return pl.pallas_call(
        node_kernel,
        out_shape=(
            jax.ShapeDtypeStruct((NODE, F), jnp.bfloat16),
            jax.ShapeDtypeStruct((PIECE, CH), jnp.float32),
        ),
        in_specs=[vmem] * 3,
        out_specs=(vmem, vmem),
        compiler_params=pltpu.CompilerParams(vmem_limit_bytes=8 * 1024 * 1024),
        cost_estimate=pl.CostEstimate(
            flops=2 * NODE * CH * F, bytes_accessed=1024 * 1024, transcendentals=NODE
        ),
        name="node_stage",
    )(parts, degree, weight)


def exchange(parts, axes):
    return lax.all_to_all(parts, axes, 0, 0)


def spread(piece, axes, n):
    return exchange(jnp.broadcast_to(piece[None], (n,) + piece.shape), axes)


def swap_cores(block):
    return lax.ppermute(block, "core", [(0, 1), (1, 0)])


def shifted(block, axis, n, shift):
    return lax.ppermute(block, axis, [(i, (i + shift) % n) for i in range(n)])


def per_device(features, out_degree, in_degree, tile_pos, tile_count, tiles, weight, cotangent):
    core = lax.axis_index("core")
    place = jnp.stack([lax.axis_index("x"), lax.axis_index("zl")])
    over_z = exchange(scaled_copies(features[0], out_degree), "zh")
    copies = jnp.broadcast_to(over_z[None], (Y,) + over_z.shape)
    copies, cotangent, in_degree, tile_pos = lax.optimization_barrier(
        (copies, cotangent, in_degree, tile_pos)
    )
    source = exchange(copies, "y")

    scaled_cot = (
        cotangent.astype(jnp.float32) * lax.rsqrt(in_degree.astype(jnp.float32))[:, :, None]
    ).astype(jnp.bfloat16)
    over_zl = jnp.concatenate(
        [scaled_cot] + [shifted(scaled_cot, "zl", Z_LO, s) for s in range(1, Z_LO)]
    )
    cotangents = [over_zl] + [shifted(over_zl, "x", X, s) for s in range(1, X)]
    places = tile_pos[0, 0, :, 0] * COL_TILES + tile_pos[0, 0, :, 1]
    source, places, *cotangents = lax.optimization_barrier((source, places, *cotangents))

    keep, send = tile_product(
        places, tile_count[0], core.reshape(1), tiles[0, 0], source
    )
    arrived = swap_cores(send)
    parts = exchange(pair_stage(place, keep, arrived, cotangents), ("zl", "x"))

    output, piece = node_stage(parts, in_degree[0][:, None], weight)

    halves = jnp.broadcast_to(
        piece.astype(jnp.bfloat16).reshape(1, CORE, PIECE // CORE, CH),
        (Y, CORE, PIECE // CORE, CH),
    ).reshape(Y * CORE, PIECE // CORE, CH)
    piece = jnp.sum(exchange(halves, ("y", "core")).astype(jnp.float32), axis=0)
    piece = lax.psum(piece.astype(jnp.bfloat16), "zh")
    pieces = spread(piece, ("zl", "x", "core"), CORE * ROW_TILES)
    grad = pieces[: CORE * F // PIECE].reshape(F // CH, CH, CH).astype(jnp.float32)
    grad_weight = jnp.concatenate([grad[k] for k in range(F // CH)], axis=1)
    return (output[None], grad_weight)


def solution(mesh):
    fine = Mesh(mesh.devices.reshape(Z_HI, Y, X, Z_LO, CORE), ROW + COL)
    return jax.shard_map(
        per_device,
        mesh=fine,
        in_specs=(
            P(COL, ROW, None),
            P(COL, ROW),
            P(ROW, COL),
            P(ROW, COL, None, None),
            P(ROW, COL),
            P(ROW, COL, None, None, None),
            P(),
            P(ROW, COL, None),
        ),
        out_specs=(P(ROW, COL, None), P()),
        check_vma=False,
    )
```
